256 devices in a mesh: grp: 8 (over y, core), dev: 32 (over x, z).
Axes of the slice: x: 4, y: 4, z: 8, core: 2. Of those that a mesh axis runs over, the one named last changes fastest.
Arguments:
- features: bfloat16 [512, 128, 768], P(('grp', 'dev'))
- tile_counts: int32 [512], P(('grp', 'dev')), may hold values from 20 to 120
- projection: bfloat16 [768, 512], replicated, may hold values from -0.21875 to 0.21875
Outputs:
- tile_maxima: float32 [512, 512, 128], P('grp', 'dev')
- chamfer: float32 [512, 512], P('grp', 'dev')
The draws below stay inside these ranges and needn't reach their ends.
All inputs are finite; a program needn't handle non-finite values.
Results may differ from the reference program's by a relative error of at most 0.0014.
Values may be sent and summed in bfloat16 or wider, within the bound.
A program may use at most 64 MiB of HBM per device.

```python
import jax
import jax.numpy as jnp
from jax import lax

P_SIZE = 128
F = 768
E = 512
SLIDES = 512


def draw_features(key, part):
    key = jax.random.fold_in(key, 11)
    key_base, key_pair, key_mix = jax.random.split(key, 3)
    base = jax.random.normal(key_base, (SLIDES, P_SIZE, F), jnp.float32)
    partner = jax.random.permutation(key_pair, SLIDES)
    mix = jax.random.uniform(key_mix, (SLIDES, 1, 1), jnp.float32, 0.3, 1.2)
    copied = jnp.roll(base[partner], 1, axis=1)
    return jnp.clip(base + mix * copied, -6.0, 6.0).astype(jnp.bfloat16)


def place_ends(values, stream_key, low, largest):
    extent = values.shape
    place = [jax.random.randint(jax.random.fold_in(stream_key, axis), (), 0, extent[axis]) for axis in range(len(extent))]
    values = values.at[tuple(place)].set(low)
    longest = extent.index(max(extent))
    place[longest] = (place[longest] + 1) % extent[longest]
    return values.at[tuple(place)].set(largest)


def normal_values(rng, extent, spread, bound, kind=jnp.bfloat16):
    return jnp.clip(spread * jax.random.normal(rng, extent, jnp.float32), -bound, bound).astype(kind)


def setup_inputs(seed: int = 0) -> dict:
    arg_keys = jax.random.split(jax.random.key(seed), 4)
    features = draw_features(jax.random.fold_in(arg_keys[3], 71), 0)
    tile_counts = place_ends(jax.random.randint(arg_keys[1], (SLIDES,), P_SIZE * 5 // 32, P_SIZE * 15 // 16 + 1), jax.random.fold_in(arg_keys[1], 1), P_SIZE * 5 // 32, (P_SIZE * 15 // 16 + 1) - 1).astype(jnp.int32)
    projection = normal_values(arg_keys[2], (F, E), F ** -0.5, 0.21875)
    return dict(features=features, tile_counts=tile_counts, projection=projection)


def embed_tiles(features, projection):
    count, slots, width = features.shape
    raw = jnp.dot(features.reshape(count * slots, width), projection, preferred_element_type=jnp.float32)
    scale = lax.rsqrt(lax.optimization_barrier(jnp.sum(raw * raw, axis=1, keepdims=True)) + 1e-06)
    return (raw * scale).astype(jnp.bfloat16).reshape(count, slots, -1)

def score_block(rows, row_counts, cols, col_counts):
    slots = rows.shape[1]
    position = jnp.arange(slots, dtype=jnp.int32)
    row_valid = position[None, :] < row_counts[:, None]
    col_valid = position[None, :] < col_counts[:, None]
    score = jnp.einsum('ape,bqe->abpq', rows.astype(jnp.float32), cols.astype(jnp.float32))
    forward = lax.optimization_barrier(jnp.max(jnp.where(col_valid[None, :, None, :], score, -4.0), axis=3))
    forward = jnp.where(row_valid[:, None, :], forward, 0.0)
    back = lax.optimization_barrier(jnp.max(jnp.where(row_valid[:, None, :, None], score, -4.0), axis=2))
    back = jnp.where(col_valid[None, :, :], back, 0.0)
    row_mean = lax.optimization_barrier(jnp.sum(forward, axis=2)) / row_counts[:, None].astype(jnp.float32)
    col_mean = lax.optimization_barrier(jnp.sum(back, axis=2)) / col_counts[None, :].astype(jnp.float32)
    return (forward, 0.5 * (row_mean + col_mean))

def reference(features, tile_counts, projection):
    embed = embed_tiles(features, projection)
    total = embed.shape[0]
    group = 4
    rows = embed.reshape(total // group, group, embed.shape[1], embed.shape[2])
    counts = tile_counts.reshape(total // group, group)

    def one_block(pair):
        return score_block(pair[0], pair[1], embed, tile_counts)
    forward, chamfer = lax.map(one_block, (rows, counts))
    tile_maxima = forward.reshape(total, total, embed.shape[1])
    return (tile_maxima, chamfer.reshape(total, total))
```

```python
import functools

import jax
import jax.numpy as jnp
from jax import lax
from jax.experimental import pallas as pl
from jax.experimental.pallas import tpu as pltpu
from jax.sharding import PartitionSpec as P

MESH = pl.DeviceIdType.MESH

NX, NY, NZ = 4, 4, 8
SLOTS = 128
KEEP = 120
SHARD = 2 * KEEP
CUT = (0, 128, SHARD)

PLUS = ((0, 3, 0), (1, 3, 0), (0, 2, 0), (1, 3, 3), (1, 3, 1), (1, 2, 0), (1, 3, 2), (1, 2, 1))
MINUS = ((0, 1, 0), (1, 1, 0), (1, 1, 1), (1, 1, 3), (1, 1, 2), (1, 2, 3), (1, 2, 2))


def swapped(pieces):
    return tuple((1 - piece, oy, ox) for piece, ox, oy in pieces)


LINKS = {(1, 0): PLUS, (-1, 0): MINUS, (0, 1): swapped(PLUS), (0, -1): swapped(MINUS)}


def sends_of(piece, ox, oy):
    out = []
    for (dx, dy), pieces in LINKS.items():
        if (piece, (ox - dx) % NX, (oy - dy) % NY) in pieces:
            out.append((dx, dy))
    return out


def arrivals():
    rounds = []
    for turn in range(max(len(p) for p in LINKS.values())):
        rounds.append([(d, p[turn]) for d, p in LINKS.items() if turn < len(p)])
    return rounds


def kernel(features, counts, projection, out, chamfer, emb, mine, rows, cols, best, gsum, gsumt, gline, gback, *sems):
    (row_send, row_recv, col_send, col_recv, twin_send, twin_recv, shuf_send, shuf_recv, out_send, out_recv, line_send, line_recv, back_send, back_recv) = sems
    grp, dev = lax.axis_index("grp"), lax.axis_index("dev")
    y, c = grp // 2, grp % 2
    x, z = dev // NZ, dev % NZ
    sign = 1 - 2 * c

    def device(x, y, z, c):
        return (y * 2 + c, x * NZ + z)

    def near(dx=0, dy=0, dz=0):
        return device((x + sign * dx + NX) % NX, (y + sign * dy + NY) % NY, (z + sign * dz + NZ) % NZ, c)

    twin = device(x, y, z, 1 - c)
    shuffle_to = device(z % NX, y, x + NX * c, z // NX)
    shuffle_self = z == x + NX * c
    special = jnp.logical_and(shuffle_self, x == y)

    barrier = pltpu.get_barrier_semaphore()

    def greet(target):
        pl.semaphore_signal(barrier, inc=1, device_id=target, device_id_type=MESH)

    for k in range(NX):
        @pl.when(jnp.logical_not(jnp.logical_and(special, z % NX == k)))
        def _():
            greet(device(z % NX, x, k + NX * c, z // NX))

    @pl.when(jnp.logical_not(shuffle_self))
    def _():
        greet(shuffle_to)

    for step in ((1, 0, 0), (-1, 0, 0), (2, 0, 0), (0, 1, 0), (0, -1, 0), (0, 0, 1), (0, 0, -1)):
        greet(near(*step))
    greet(twin)

    raw = jnp.dot(features[...].reshape(2 * SLOTS, -1), projection[...], preferred_element_type=jnp.float32)
    scale = lax.rsqrt(jnp.sum(raw * raw, axis=1, keepdims=True) + 1e-06)
    embed = (raw * scale).astype(jnp.bfloat16).astype(jnp.float32)
    slot = lax.broadcasted_iota(jnp.int32, (SLOTS, 1), 0)
    for s in range(2):
        block = embed[s * SLOTS:(s + 1) * SLOTS]
        valid = slot < counts[s]
        count = jnp.where(slot == SLOTS - 1, counts[s].astype(jnp.float32), 0.0)
        rows[z, s] = jnp.where(valid, block, count).astype(jnp.bfloat16)
        emb[pl.ds(s * KEEP, KEEP), :] = jnp.where(valid, block, block[0:1])[:KEEP]
    mine[...] = emb[...].astype(jnp.bfloat16)

    pl.semaphore_wait(barrier, 13 - shuffle_self.astype(jnp.int32) - special.astype(jnp.int32))

    pending = []

    def remote(src, dst, send, recv, target):
        copy = pltpu.make_async_remote_copy(src_ref=src, dst_ref=dst, send_sem=send, recv_sem=recv, device_id=target, device_id_type=MESH)
        copy.start()
        pending.append(copy)

    def arrived(ref, sem):
        pltpu.make_async_copy(ref, ref, sem).wait()

    def shuffle_copy(piece):
        part = pl.ds(CUT[piece], CUT[piece + 1] - CUT[piece])
        return pltpu.make_async_remote_copy(
            src_ref=mine.at[part], dst_ref=cols.at[z // NX, y, z % NX, part],
            send_sem=shuf_send.at[piece], recv_sem=shuf_recv.at[piece], device_id=shuffle_to, device_id_type=MESH)

    @pl.when(jnp.logical_not(shuffle_self))
    def _():
        shuffle_copy(0).start()
        shuffle_copy(1).start()

    @pl.when(shuffle_self)
    def _():
        cols[c, y, x] = mine[...]

    ring_index = {}

    def ring_send(offset, half, way):
        key = ((offset - way), half)
        index = ring_index.setdefault(key, len(ring_index))
        ref = rows.at[(z + sign * offset + NZ) % NZ, half]
        remote(ref, ref, row_send.at[index], row_recv.at[index], near(0, 0, way))

    def ring_wait(offset, half):
        arrived(rows.at[(z + sign * offset + NZ) % NZ, half], row_recv.at[ring_index[(offset, half)]])

    for half in range(2):
        for way in (1, -1):
            ring_send(0, half, way)

    col_index = {}

    def col_ref(piece, ox, oy):
        part = pl.ds(CUT[piece], CUT[piece + 1] - CUT[piece])
        return cols.at[c, (y + sign * oy + NY) % NY, (x + sign * ox + NX) % NX, part]

    def col_key(piece, ox, oy):
        return col_index.setdefault((piece, ox % NX, oy % NY), len(col_index))

    def pass_on(piece, ox, oy):
        for dx, dy in sends_of(piece, ox, oy):
            index = col_key(piece, ox - dx, oy - dy)
            ref = col_ref(piece, ox, oy)
            remote(ref, ref, col_send.at[index], col_recv.at[index], near(dx, dy, 0))

    def to_twin(ox, oy):
        index = ox * NY + oy
        ref = cols.at[c, (y + sign * oy + NY) % NY, (x + sign * ox + NX) % NX]
        remote(ref, ref, twin_send.at[index], twin_recv.at[index], twin)

    def from_twin(ox, oy):
        index = (-ox % NX) * NY + (-oy % NY)
        arrived(cols.at[1 - c, (y + sign * oy + NY) % NY, (x + sign * ox + NX) % NX], twin_recv.at[index])

    for piece in range(2):
        @pl.when(jnp.logical_not(shuffle_self))
        def _():
            shuffle_copy(piece).wait_recv()

        pass_on(piece, 0, 0)
    to_twin(0, 0)

    have = {}
    ring_order = [[(o * way, h) for way in (-1, 1)] for o in (1, 2, 3) for h in (0, 1)] + [[(-4, 0), (4, 1)]]
    for turn, pieces in enumerate(arrivals()):
        for _, (piece, ox, oy) in pieces:
            arrived(col_ref(piece, ox, oy), col_recv.at[col_key(piece, ox, oy)])
            pass_on(piece, ox, oy)
            have.setdefault((ox, oy), []).append(piece)
            if len(have[(ox, oy)]) == 2:
                to_twin(ox, oy)
        if turn < len(ring_order):
            for offset, half in ring_order[turn]:
                ring_wait(offset, half)
                way = 1 if offset < 0 else -1
                if abs(offset) < 3 or (abs(offset) == 3 and half == (0 if way == 1 else 1)):
                    ring_send(offset, half, way)
    for ox in range(NX):
        for oy in range(NY):
            from_twin(ox, oy)

    lane = lax.broadcasted_iota(jnp.int32, (1, SLOTS), 1)

    def unit(i, carry):
        column, half = i // 2, i % 2
        block = cols[half, column].reshape(NX * SHARD, -1)
        for ring in range(NZ):
            score = lax.dot_general(block, rows[ring].reshape(2 * SLOTS, -1), (((1,), (1,)), ((), ())), preferred_element_type=jnp.float32)
            top = jnp.max(score.reshape(2 * NX, KEEP, 2 * SLOTS), axis=1)
            for s in range(2):
                best[column, 2 * ring + s, pl.ds(pl.multiple_of(half * 8, 8), 8), :] = jnp.where(lane < KEEP, top[:, s * SLOTS:(s + 1) * SLOTS], 0.0)
        return carry

    lax.fori_loop(0, 2 * NY, unit, 0)

    for column in range(NY):
        for ring in range(NZ):
            for s in range(2):
                a = 2 * ring + s
                count = rows[ring, s, pl.ds(SLOTS - 16, 16), 0:1].astype(jnp.float32)[15:16]
                gsumt[column, :, a:a + 1] = jnp.sum(best[column, a], axis=1, keepdims=True) / count
        gsum[column, :, 0:16] = gsumt[column, :, 0:16].T

    def back_copy(k):
        return pltpu.make_async_remote_copy(
            src_ref=gsumt.at[k], dst_ref=gback.at[z % NX], send_sem=back_send.at[k], recv_sem=back_recv.at[z % NX],
            device_id=device(y, k, x + NX * c, z // NX), device_id_type=MESH)

    for k in range(NY):
        here = jnp.logical_and(special, y == k)

        @pl.when(jnp.logical_not(here))
        def _():
            back_copy(k).start()

        @pl.when(here)
        def _():
            gback[z % NX] = gsumt[k]

    for d in (1, 3, 2):
        column = (x + d) % NX
        to = device(column, y, z, c)
        remote(gsum.at[column], gline.at[x], line_send.at[d], line_recv.at[d], to)
        remote(best.at[column], out.at[pl.ds(16 * x, 16)], out_send.at[d], out_recv.at[d], to)
    gline[x] = gsum[x]
    out[pl.ds(16 * x, 16)] = best[x]

    for d in (1, 3, 2):
        source = (x - d + NX) % NX
        arrived(gline.at[source], line_recv.at[d])
    for k in range(NX):
        @pl.when(jnp.logical_not(jnp.logical_and(special, z % NX == k)))
        def _():
            arrived(gback.at[k], back_recv.at[k])
    for k in range(NX):
        chamfer[pl.ds(16 * k, 16), :] = 0.5 * (gline[k][:, 0:16] + gback[k][:, 0:16])
    for d in (1, 3, 2):
        source = (x - d + NX) % NX
        arrived(out.at[pl.ds(16 * source, 16)], out_recv.at[d])

    for copy in pending:
        copy.wait_send()

    @pl.when(jnp.logical_not(shuffle_self))
    def _():
        shuffle_copy(0).wait_send()
        shuffle_copy(1).wait_send()

    for k in range(NY):
        @pl.when(jnp.logical_not(jnp.logical_and(special, y == k)))
        def _():
            back_copy(k).wait_send()


def on_device(features, tile_counts, projection):
    dma = pltpu.SemaphoreType.DMA
    width = projection.shape[1]
    vmem = pl.BlockSpec(memory_space=pltpu.VMEM)
    return pl.pallas_call(
        kernel,
        name="chamfer",
        out_shape=(jax.ShapeDtypeStruct((64, 16, SLOTS), jnp.float32), jax.ShapeDtypeStruct((64, 16), jnp.float32)),
        in_specs=[vmem, pl.BlockSpec(memory_space=pltpu.SMEM), vmem],
        out_specs=(vmem, vmem),
        scratch_shapes=[
            pltpu.VMEM((SHARD, width), jnp.float32),
            pltpu.VMEM((SHARD, width), jnp.bfloat16),
            pltpu.VMEM((NZ, 2, SLOTS, width), jnp.bfloat16),
            pltpu.VMEM((2, NY, NX, SHARD, width), jnp.bfloat16),
            pltpu.VMEM((NY, 16, 16, SLOTS), jnp.float32),
            pltpu.VMEM((NY, 16, SLOTS), jnp.float32),
            pltpu.VMEM((NY, 16, SLOTS), jnp.float32),
            pltpu.VMEM((NX, 16, SLOTS), jnp.float32),
            pltpu.VMEM((NX, 16, SLOTS), jnp.float32),
            dma((14,)), dma((14,)), dma((30,)), dma((30,)), dma((16,)), dma((16,)), dma((2,)), dma((2,)),
            dma((4,)), dma((4,)), dma((4,)), dma((4,)), dma((4,)), dma((4,)),
        ],
        compiler_params=pltpu.CompilerParams(collective_id=0, has_side_effects=True, vmem_limit_bytes=48 * 2**20),
    )(features, tile_counts, projection)


def solution(mesh):
    return jax.shard_map(
        on_device,
        mesh=mesh,
        in_specs=(P(("grp", "dev"), None, None), P(("grp", "dev")), P()),
        out_specs=(P("grp", "dev", None), P("grp", "dev")),
        check_vma=False,
    )
```

```python
import jax
import jax.numpy as jnp
from jax import lax
from jax.experimental import pallas as pl
from jax.experimental.pallas import tpu as pltpu
from jax.sharding import PartitionSpec as P

MESH = pl.DeviceIdType.MESH

NX, NY, NZ = 4, 4, 8
SLOTS = 128
KEEP = 120
SHARD = 2 * KEEP
PIECES = ((0, 0, 128), (1, 128, 240))

T_RING, D_RING = 1.5, 2.75
T_COL, D_COL = 1.5, 2.9
T_TWIN = 1.5
T_TILE, T_BLOCK = 0.075, 0.1


def per_piece(entries):
    return tuple((p, ox, oy) for way, ox, oy in entries for p, piece in enumerate(PIECES) if piece[0] == way)


PLUS = ((0, 3, 0), (1, 3, 0), (0, 2, 0), (1, 3, 3), (1, 3, 1), (1, 2, 0), (1, 3, 2), (1, 2, 1))
MINUS = ((0, 1, 0), (1, 1, 0), (1, 1, 1), (1, 1, 3), (1, 1, 2), (1, 2, 3), (1, 2, 2))


def swapped(entries):
    return tuple((1 - way, oy, ox) for way, ox, oy in entries)


LINKS = {(1, 0): per_piece(PLUS), (-1, 0): per_piece(MINUS), (0, 1): per_piece(swapped(PLUS)), (0, -1): per_piece(swapped(MINUS))}
MOST = 8
WAY_PIECES = max(sum(1 for p in PIECES if p[0] == way) for way in range(2))


def sends_of(p, ox, oy):
    return [(dx, dy) for (dx, dy), pieces in LINKS.items() if (p, (ox - dx) % NX, (oy - dy) % NY) in pieces]


def plan():
    times = {}
    for pieces in LINKS.values():
        for i, key in enumerate(pieces):
            times[key] = T_COL + D_COL * (i + 1) / WAY_PIECES
    events = [(t, "col", key) for key, t in times.items()]
    for p in range(len(PIECES)):
        times[(p, 0, 0)] = 0.0
    ready = {}
    for ox in range(NX):
        for oy in range(NY):
            t = max(times[(p, ox, oy)] for p in range(len(PIECES)))
            twin = (1, -ox % NX, -oy % NY)
            ready[(0, ox, oy)] = t
            ready[twin] = t + T_TWIN
            events.append((t + 0.001, "to_twin", (ox, oy)))
            events.append((t + T_TWIN, "twin", twin[1:]))
    tile_ready = {0: 0.0}
    for slot, halves in enumerate([[(o * way, h) for way in (-1, 1)] for o in (1, 2, 3) for h in (0, 1)] + [[(-4, 0), (4, 1)]]):
        for offset, half in halves:
            t = T_RING + D_RING * (slot + 1)
            events.append((t, "ring", (offset, half)))
            tile = 4 if abs(offset) == 4 else offset
            tile_ready[tile] = max(t, tile_ready.get(tile, 0.0))
    events.sort(key=lambda e: e[0])
    todo = {shard: set(tile_ready) for shard in ready}
    order = [(core, oy) for oy in (0, 3, 1, 2) for core in (0, 1)]
    program, now = [], 0.0
    while events or todo:
        while events and events[0][0] <= now:
            program.append(("event",) + events.pop(0)[1:])
            now += 0.05
        best = None
        for shard, tiles in todo.items():
            if ready[shard] > now:
                continue
            usable = sorted(t for t in tiles if tile_ready[t] <= now)
            if not usable or (len(usable) < 2 and len(usable) < len(tiles)):
                continue
            if events:
                usable = usable[:MOST]
            rank = (len(usable) == len(tiles), -order.index((shard[0], shard[2])), len(usable))
            if best is None or rank > best[0]:
                best = (rank, shard, usable)
        if best is None:
            now = max(now, events[0][0])
            continue
        _, shard, usable = best
        program.append(("block", shard, tuple(usable)))
        now += T_BLOCK + T_TILE * len(usable)
        todo[shard] -= set(usable)
        if not todo[shard]:
            del todo[shard]
            program.append(("done", shard))
            now += 0.1
    return program, now


def kernel(features_hbm, counts, projection_hbm, taken, back, features, projection, emb, rows, cols, best, count, means, *sems):
    load, row_send, row_recv, col_send, col_recv, twin_send, twin_recv, out_send, out_recv, back_send, back_recv = sems
    grp, dev = lax.axis_index("grp"), lax.axis_index("dev")
    y, c = grp // 2, grp % 2
    x, z = dev // NZ, dev % NZ
    sign = 1 - 2 * c

    def device(x, y, z, c):
        return (y * 2 + c, x * NZ + z)

    def near(dx=0, dy=0, dz=0):
        return device((x + sign * dx + NX) % NX, (y + sign * dy + NY) % NY, (z + sign * dz + NZ) % NZ, c)

    twin = device(x, y, z, 1 - c)
    special = jnp.logical_and(z == x + NX * c, x == y)

    barrier = pltpu.get_barrier_semaphore()

    def greet(target):
        pl.semaphore_signal(barrier, inc=1, device_id=target, device_id_type=MESH)

    def back_source(k):
        return jnp.logical_and(special, z == k)

    for k in range(NZ):
        @pl.when(jnp.logical_not(back_source(k)))
        def _():
            greet(device(z % NX, x, k, z // NX))

    for dx in range(NX):
        for dz in range(NZ):
            if (dx, dz) != (0, 0):
                greet(device((x + dx) % NX, y, (z + dz) % NZ, c))
    greet(near(0, 1, 0))
    greet(near(0, -1, 0))
    greet(twin)

    load_features = pltpu.make_async_copy(features_hbm, features, load.at[0])
    load_projection = pltpu.make_async_copy(projection_hbm, projection, load.at[1])
    load_features.start()
    load_projection.start()
    load_features.wait()
    load_projection.wait()

    raw = jnp.dot(features[...].reshape(2 * SLOTS, -1), projection[...], preferred_element_type=jnp.float32)
    scale = lax.rsqrt(jnp.sum(raw * raw, axis=1, keepdims=True) + 1e-06)
    embed = (raw * scale).astype(jnp.bfloat16).astype(jnp.float32)
    slot = lax.broadcasted_iota(jnp.int32, (SLOTS, 1), 0)
    for s in range(2):
        block = embed[s * SLOTS:(s + 1) * SLOTS]
        valid = slot < counts[s]
        number = jnp.where(slot == SLOTS - 1, counts[s].astype(jnp.float32), 0.0)
        rows[z, s] = jnp.where(valid, block, number).astype(jnp.bfloat16)
        emb[pl.ds(s * KEEP, KEEP), :] = jnp.where(valid, block, block[0:1])[:KEEP]
    cols[y, x, c] = emb[...].astype(jnp.bfloat16)
    means[...] = jnp.zeros_like(means)

    pl.semaphore_wait(barrier, (NX * NZ - 1) + 3 + NZ - special.astype(jnp.int32))

    pending = []

    def remote(src, dst, send, recv, target):
        copy = pltpu.make_async_remote_copy(src_ref=src, dst_ref=dst, send_sem=send, recv_sem=recv, device_id=target, device_id_type=MESH)
        copy.start()
        pending.append(copy)

    def arrived(ref, sem):
        pltpu.make_async_copy(ref, ref, sem).wait()

    ring_index = {}

    def ring_ref(offset, half):
        return rows.at[(z + sign * offset + NZ) % NZ, half]

    def ring_send(offset, half, way):
        index = ring_index.setdefault((offset - way, half), len(ring_index))
        ref = ring_ref(offset, half)
        remote(ref, ref, row_send.at[index], row_recv.at[index], near(0, 0, way))

    def ring_event(offset, half):
        arrived(ring_ref(offset, half), row_recv.at[ring_index[(offset, half)]])
        way = 1 if offset < 0 else -1
        if abs(offset) < 3 or (abs(offset) == 3 and half == (0 if way == 1 else 1)):
            ring_send(offset, half, way)

    col_index = {}

    def place(core, ox, oy):
        return (y + sign * oy + NY) % NY, (x + sign * ox + NX) % NX, (c if core == 0 else 1 - c)

    def col_ref(p, ox, oy):
        return cols.at[(*place(0, ox, oy), pl.ds(PIECES[p][1], PIECES[p][2] - PIECES[p][1]))]

    def col_key(p, ox, oy):
        return col_index.setdefault((p, ox % NX, oy % NY), len(col_index))

    def pass_on(p, ox, oy):
        for dx, dy in sends_of(p, ox, oy):
            index = col_key(p, ox - dx, oy - dy)
            ref = col_ref(p, ox, oy)
            remote(ref, ref, col_send.at[index], col_recv.at[index], near(dx, dy, 0))

    def col_event(p, ox, oy):
        arrived(col_ref(p, ox, oy), col_recv.at[col_key(p, ox, oy)])
        pass_on(p, ox, oy)

    def to_twin_event(ox, oy):
        index = ox * NY + oy
        ref = cols.at[place(0, ox, oy)]
        remote(ref, ref, twin_send.at[index], twin_recv.at[index], twin)

    def twin_event(ox, oy):
        arrived(cols.at[place(1, ox, oy)], twin_recv.at[(-ox % NX) * NY + (-oy % NY)])

    def block_step(core, ox, oy, tiles):
        where = place(core, ox, oy)
        block = cols[where]
        for tile in tiles:
            ring = (z + sign * tile + NZ) % NZ
            score = lax.dot_general(block, rows[ring].reshape(2 * SLOTS, -1), (((1,), (1,)), ((), ())), preferred_element_type=jnp.float32)
            for b in range(2):
                top = jnp.max(score[b * KEEP:(b + 1) * KEEP], axis=0, keepdims=True)
                for s in range(2):
                    best[(*where, b, pl.ds(2 * ring + s, 1))] = top[:, s * SLOTS:(s + 1) * SLOTS]

    lane = lax.broadcasted_iota(jnp.int32, (1, SLOTS), 1)

    def out_copy(core, ox, oy):
        column, line, half = place(core, ox, oy)
        index = (core * NX + ox) * NY + oy
        return pltpu.make_async_remote_copy(
            src_ref=best.at[column, line, half], dst_ref=taken.at[x, z], send_sem=out_send.at[index], recv_sem=out_recv.at[x * NZ + z],
            device_id=device(column, y, line + NX * half, c), device_id_type=MESH)

    def out_here(core, ox, oy):
        column, line, half = place(core, ox, oy)
        return jnp.logical_and(column == x, line + NX * half == z)

    def back_copy(core, oy):
        column, _, half = place(core, 0, oy)
        return pltpu.make_async_remote_copy(
            src_ref=means.at[column, half], dst_ref=back.at[z], send_sem=back_send.at[core * NY + oy], recv_sem=back_recv.at[z],
            device_id=device(y, column, x + NX * c, half), device_id_type=MESH)

    def back_here(core, oy):
        column, _, half = place(core, 0, oy)
        return jnp.logical_and(special, jnp.logical_and(column == y, half == c))

    finished = {}

    def done_step(core, ox, oy):
        if not finished:
            for a in range(2 * NZ):
                count[a:a + 1] = rows[a // 2, a % 2, pl.ds(SLOTS - 16, 16), 0:SLOTS].astype(jnp.float32)[15:16]
        where = place(core, ox, oy)
        column, line, half = where
        mean = means[column, half]
        for b in range(2):
            top = jnp.where(lane < KEEP, best[(*where, b)], 0.0)
            value = jnp.sum(top, axis=1, keepdims=True) / count[...]
            best[(*where, b)] = jnp.where(lane == SLOTS - 1, value, top)
            mean = jnp.where(lane == 2 * line + b, value, mean)
        means[column, half] = mean

        @pl.when(jnp.logical_not(out_here(core, ox, oy)))
        def _():
            out_copy(core, ox, oy).start()

        @pl.when(out_here(core, ox, oy))
        def _():
            taken[x, z] = best[where]

        group = finished.setdefault((core, oy), [])
        group.append(ox)
        if len(group) == NX:
            @pl.when(jnp.logical_not(back_here(core, oy)))
            def _():
                back_copy(core, oy).start()

            @pl.when(back_here(core, oy))
            def _():
                back[z] = means[column, half]

    for p in range(len(PIECES)):
        pass_on(p, 0, 0)
        if p == 0:
            for half in range(2):
                for way in (1, -1):
                    ring_send(0, half, way)
    handlers = {"col": col_event, "ring": ring_event, "to_twin": to_twin_event, "twin": twin_event}
    for entry in plan()[0]:
        if entry[0] == "event":
            handlers[entry[1]](*entry[2])
        elif entry[0] == "block":
            block_step(*entry[1], entry[2])
        else:
            done_step(*entry[1])

    for k in range(NZ):
        @pl.when(jnp.logical_not(back_source(k)))
        def _():
            arrived(back.at[k], back_recv.at[k])
    for i in range(NX):
        for k in range(NZ):
            @pl.when(jnp.logical_not(jnp.logical_and(x == i, z == k)))
            def _():
                arrived(taken.at[i, k], out_recv.at[i * NZ + k])

    for copy in pending:
        copy.wait_send()
    for core in range(2):
        for oy in range(NY):
            @pl.when(jnp.logical_not(back_here(core, oy)))
            def _():
                back_copy(core, oy).wait_send()

            for ox in range(NX):
                @pl.when(jnp.logical_not(out_here(core, ox, oy)))
                def _():
                    out_copy(core, ox, oy).wait_send()


def place_kernel(taken, back, out, chamfer, turned):
    lane = lax.broadcasted_iota(jnp.int32, (1, SLOTS), 1)
    for k in range(NZ):
        turned[...] = back[k].T
        for i in range(NX):
            chamfer[pl.ds(16 * i + 2 * k, 2), :] = turned[pl.ds(2 * i, 2), :]
    for i in range(NX):
        line = jnp.zeros((16, SLOTS), jnp.float32)
        for k in range(NZ):
            for b in range(2):
                value = taken[i, k, b]
                line = jnp.where(lane == 2 * k + b, value[:, SLOTS - 1:SLOTS], line)
                out[pl.ds(16 * i, 16), 2 * k + b, :] = jnp.where(lane < KEEP, value, 0.0)
        part = pl.ds(16 * i, 16)
        chamfer[part, :] = 0.5 * (chamfer[part, :] + line[:, 0:16])


def on_device(features, tile_counts, projection):
    dma = pltpu.SemaphoreType.DMA
    width = projection.shape[1]
    vmem = pl.BlockSpec(memory_space=pltpu.VMEM)
    anywhere = pl.BlockSpec(memory_space=pl.ANY)
    pieces = len(PIECES)
    f32 = jnp.float32
    taken, back = pl.pallas_call(
        kernel,
        name="compare",
        out_shape=(jax.ShapeDtypeStruct((NX, NZ, 2, 16, SLOTS), f32), jax.ShapeDtypeStruct((NZ, 16, SLOTS), f32)),
        in_specs=[anywhere, pl.BlockSpec(memory_space=pltpu.SMEM), anywhere],
        out_specs=(vmem, vmem),
        scratch_shapes=[
            pltpu.VMEM(features.shape, jnp.bfloat16),
            pltpu.VMEM(projection.shape, jnp.bfloat16),
            pltpu.VMEM((SHARD, width), f32),
            pltpu.VMEM((NZ, 2, SLOTS, width), jnp.bfloat16),
            pltpu.VMEM((NY, NX, 2, SHARD, width), jnp.bfloat16),
            pltpu.VMEM((NY, NX, 2, 2, 16, SLOTS), f32),
            pltpu.VMEM((16, SLOTS), f32),
            pltpu.VMEM((NY, 2, 16, SLOTS), f32),
            dma((2,)), dma((14,)), dma((14,)), dma((15 * pieces,)), dma((15 * pieces,)), dma((16,)), dma((16,)),
            dma((32,)), dma((32,)), dma((8,)), dma((8,)),
        ],
        compiler_params=pltpu.CompilerParams(collective_id=0, has_side_effects=True, vmem_limit_bytes=56 * 2**20),
    )(features, tile_counts, projection)
    return pl.pallas_call(
        place_kernel,
        name="place",
        out_shape=(jax.ShapeDtypeStruct((64, 16, SLOTS), f32), jax.ShapeDtypeStruct((64, 16), f32)),
        in_specs=[vmem, vmem],
        out_specs=(vmem, vmem),
        scratch_shapes=[pltpu.VMEM((SLOTS, 16), f32)],
    )(taken, back)


def solution(mesh):
    return jax.shard_map(
        on_device,
        mesh=mesh,
        in_specs=(P(("grp", "dev"), None, None), P(("grp", "dev")), P()),
        out_specs=(P("grp", "dev", None), P("grp", "dev")),
        check_vma=False,
    )
```

```python
import jax
import jax.numpy as jnp
from jax import lax
from jax.experimental import pallas as pl
from jax.experimental.pallas import tpu as pltpu
from jax.sharding import PartitionSpec as P

MESH = pl.DeviceIdType.MESH

NX, NY, NZ = 4, 4, 8
SLOTS = 128
KEEP = 120
SHARD = 2 * KEEP
PIECES = ((0, 0, 64), (0, 64, 128), (1, 128, 192), (1, 192, 240))
WAYS = ((0, 128), (128, 240))
QUARTER = 128
WINDOW = 2

T_ROW = 0.0213
T_HOP = 2.5
T_TWIN = 2.2
T_TILE, T_BLOCK, T_EVENT = 0.07, 0.1, 0.02
MOST = 4


def per_piece(entries):
    return tuple((p, ox, oy) for way, ox, oy in entries for p, piece in enumerate(PIECES) if piece[0] == way)


PLUS = ((0, 3, 0), (1, 3, 0), (0, 2, 0), (1, 3, 3), (1, 3, 1), (1, 2, 0), (1, 3, 2), (1, 2, 1))
MINUS = ((0, 1, 0), (1, 1, 0), (1, 1, 1), (1, 1, 3), (1, 1, 2), (1, 2, 3), (1, 2, 2))


def swapped(entries):
    return tuple((1 - way, oy, ox) for way, ox, oy in entries)


def ring_order(way):
    quarters = 2 * SLOTS // QUARTER
    whole = [(-way * o, q) for o in (1, 2, 3) for q in range(quarters)]
    return tuple(whole + [(4, q) for q in range(quarters) if (q < quarters // 2) == (way == 1)])


LINKS = {
    (1, 0, 0): tuple(("col", *k) for k in per_piece(PLUS)),
    (-1, 0, 0): tuple(("col", *k) for k in per_piece(MINUS)),
    (0, 1, 0): tuple(("col", *k) for k in per_piece(swapped(PLUS))),
    (0, -1, 0): tuple(("col", *k) for k in per_piece(swapped(MINUS))),
    (0, 0, 1): tuple(("row", *k) for k in ring_order(1)),
    (0, 0, -1): tuple(("row", *k) for k in ring_order(-1)),
}


def at_sender(link, key):
    dx, dy, dz = link
    if key[0] == "row":
        offset = key[1] + dz
        return ("row", offset - NZ if offset > 4 else offset, key[2])
    return ("col", key[1], (key[2] + dx) % NX, (key[3] + dy) % NY)


def length(key):
    return QUARTER if key[0] == "row" else PIECES[key[1]][2] - PIECES[key[1]][1]


def transfers():
    time = {("row", 0, q): 0.0 for q in range(2 * SLOTS // QUARTER)}
    time.update({("col", p, 0, 0): 0.0 for p in range(len(PIECES))})
    sent = {link: [] for link in LINKS}
    actions = []
    while True:
        nearest = None
        for link, keys in LINKS.items():
            i = len(sent[link])
            if i == len(keys) or at_sender(link, keys[i]) not in time:
                continue
            start = max(time[at_sender(link, keys[i])], sent[link][i - WINDOW] if i >= WINDOW else 0.0)
            if nearest is None or start < nearest[0]:
                nearest = (start, link, i)
        if nearest is None:
            return actions, time
        start, link, i = nearest
        key = LINKS[link][i]
        end = max(start, sent[link][-1] if sent[link] else 0.0) + length(key) * T_ROW
        sent[link].append(end)
        time[key] = end + T_HOP
        actions.append((start, 1, "send", (link, i)))
        actions.append((time[key], 0, "arrive", (link, i)))


def plan():
    events, time = transfers()
    ready = {}
    for ox in range(NX):
        for oy in range(NY):
            for way in range(2):
                t = max(time[("col", p, ox, oy)] for p, piece in enumerate(PIECES) if piece[0] == way)
                twin = (-ox % NX, -oy % NY)
                events.append((t, 2, "to_twin", (way, ox, oy)))
                events.append((t + T_TWIN, 0, "twin", (way, *twin)))
                ready[(0, ox, oy)] = max(ready.get((0, ox, oy), 0.0), t)
                ready[(1, *twin)] = max(ready.get((1, *twin), 0.0), t + T_TWIN)
    tile_ready = {tile: max(time[("row", tile, q)] for q in range(2 * SLOTS // QUARTER)) for tile in range(-3, 5)}
    events.sort(key=lambda e: e[:2])
    todo = {shard: set(tile_ready) for shard in ready}
    order = [(core, oy) for oy in (0, 3, 1, 2) for core in (0, 1)]
    program, now, late = [], 0.0, []
    while events or todo:
        while events and events[0][0] <= now:
            program.append((events[0][2], *events.pop(0)[3]))
            now += T_EVENT
        best = None
        for shard, tiles in todo.items():
            if ready[shard] > now:
                continue
            usable = sorted(t for t in tiles if tile_ready[t] <= now)
            if not usable or (len(usable) < 2 and len(usable) < len(tiles)):
                continue
            if events:
                usable = usable[:MOST]
            rank = (len(usable) == len(tiles), -order.index((shard[0], shard[2])), len(usable))
            if best is None or rank > best[0]:
                best = (rank, shard, usable)
        if best is None:
            now = max(now, events[0][0])
            continue
        _, shard, usable = best
        program.append(("block", shard, tuple(usable)))
        now += T_BLOCK + T_TILE * len(usable)
        todo[shard] -= set(usable)
        if not todo[shard]:
            del todo[shard]
        if late:
            program.append(("ship", late.pop()))
        group = shard[0], shard[2]
        if not any((core, oy) == group for core, _, oy in todo):
            program.append(("finish", group))
            late.append(group)
            now += 0.3
    program.append(("ship", late.pop()))
    return program, now


def kernel(features_hbm, counts, projection_hbm, taken, back, features, projection, emb, rows, cols, best, count, means, *sems):
    load, link_send, link_recv, twin_send, twin_recv, out_send, out_recv, back_send, back_recv = sems
    grp, dev = lax.axis_index("grp"), lax.axis_index("dev")
    y, c = grp // 2, grp % 2
    x, z = dev // NZ, dev % NZ
    sign = 1 - 2 * c

    def device(x, y, z, c):
        return (y * 2 + c, x * NZ + z)

    def near(dx=0, dy=0, dz=0):
        return device((x + sign * dx + NX) % NX, (y + sign * dy + NY) % NY, (z + sign * dz + NZ) % NZ, c)

    twin = device(x, y, z, 1 - c)
    special = jnp.logical_and(z == x + NX * c, x == y)

    barrier = pltpu.get_barrier_semaphore()

    def greet(target):
        pl.semaphore_signal(barrier, inc=1, device_id=target, device_id_type=MESH)

    def back_source(k):
        return jnp.logical_and(special, z == k)

    load_features = pltpu.make_async_copy(features_hbm, features, load.at[0])
    load_projection = pltpu.make_async_copy(projection_hbm, projection, load.at[1])
    load_features.start()
    load_projection.start()
    for k in range(NZ):
        @pl.when(jnp.logical_not(back_source(k)))
        def _():
            greet(device(z % NX, x, k, z // NX))

    for dx in range(NX):
        for dz in range(NZ):
            if (dx, dz) != (0, 0):
                greet(device((x + dx) % NX, y, (z + dz) % NZ, c))
    greet(near(0, 1, 0))
    greet(near(0, -1, 0))
    greet(twin)

    load_features.wait()
    load_projection.wait()

    raw = jnp.dot(features[...].reshape(2 * SLOTS, -1), projection[...], preferred_element_type=jnp.float32)
    scale = lax.rsqrt(jnp.sum(raw * raw, axis=1, keepdims=True) + 1e-06)
    embed = (raw * scale).astype(jnp.bfloat16).astype(jnp.float32)
    slot = lax.broadcasted_iota(jnp.int32, (SLOTS, 1), 0)
    for s in range(2):
        block = embed[s * SLOTS:(s + 1) * SLOTS]
        valid = slot < counts[s]
        number = jnp.where(slot == SLOTS - 1, counts[s].astype(jnp.float32), 0.0)
        rows[z, s] = jnp.where(valid, block, number).astype(jnp.bfloat16)
        emb[pl.ds(s * KEEP, KEEP), :] = jnp.where(valid, block, block[0:1])[:KEEP]
    cols[y, x, c] = emb[...].astype(jnp.bfloat16)

    pl.semaphore_wait(barrier, (NX * NZ - 1) + 3 + NZ - special.astype(jnp.int32))

    def arrived(ref, sem):
        pltpu.make_async_copy(ref, ref, sem).wait()

    def place(core, ox, oy):
        return (y + sign * oy + NY) % NY, (x + sign * ox + NX) % NX, (c if core == 0 else 1 - c)

    def piece_ref(key):
        if key[0] == "row":
            return rows.at[(z + sign * key[1] + NZ) % NZ, key[2] * QUARTER // SLOTS, pl.ds(key[2] * QUARTER % SLOTS, QUARTER)]
        _, p, ox, oy = key
        return cols.at[(*place(0, ox, oy), pl.ds(PIECES[p][1], PIECES[p][2] - PIECES[p][1]))]

    number_of = {}
    for link, keys in LINKS.items():
        for i in range(len(keys)):
            number_of[(link, i)] = len(number_of)

    def link_copy(link, i):
        ref = piece_ref(at_sender(link, LINKS[link][i]))
        index = number_of[(link, i)]
        return pltpu.make_async_remote_copy(
            src_ref=ref, dst_ref=ref, send_sem=link_send.at[index], recv_sem=link_recv.at[index], device_id=near(*link), device_id_type=MESH)

    def send_event(link, i):
        if i >= WINDOW:
            link_copy(link, i - WINDOW).wait_send()
        link_copy(link, i).start()

    def arrive_event(link, i):
        arrived(piece_ref(LINKS[link][i]), link_recv.at[number_of[(link, i)]])

    def way_ref(way, core, ox, oy):
        return cols.at[(*place(core, ox, oy), pl.ds(WAYS[way][0], WAYS[way][1] - WAYS[way][0]))]

    def to_twin_event(way, ox, oy):
        index = (way * NX + ox) * NY + oy
        ref = way_ref(way, 0, ox, oy)
        pltpu.make_async_remote_copy(
            src_ref=ref, dst_ref=ref, send_sem=twin_send, recv_sem=twin_recv.at[index], device_id=twin, device_id_type=MESH).start()

    def twin_event(way, ox, oy):
        arrived(way_ref(way, 1, ox, oy), twin_recv.at[(way * NX + -ox % NX) * NY + -oy % NY])

    counted = set()

    def count_rows(tile):
        counted.add(tile)
        ring = (z + sign * tile + NZ) % NZ
        for s in range(2):
            count[pl.ds(2 * ring + s, 1)] = rows[ring, s, pl.ds(SLOTS - 16, 16), 0:SLOTS].astype(jnp.float32)[15:16]

    def block_step(core, ox, oy, tiles):
        column, line, half = place(core, ox, oy)
        block = cols[column, line, half]
        for tile in tiles:
            if tile not in counted:
                count_rows(tile)
            ring = (z + sign * tile + NZ) % NZ
            score = lax.dot_general(block, rows[ring].reshape(2 * SLOTS, -1), (((1,), (1,)), ((), ())), preferred_element_type=jnp.float32)
            for b in range(2):
                top = jnp.max(score[b * KEEP:(b + 1) * KEEP], axis=0, keepdims=True)
                for s in range(2):
                    best[column, half, line, b, pl.ds(2 * ring + s, 1)] = top[:, s * SLOTS:(s + 1) * SLOTS]

    lane = lax.broadcasted_iota(jnp.int32, (1, SLOTS), 1)

    def group_place(core, oy):
        column, _, half = place(core, 0, oy)
        return column, half

    def out_copy(column, line, half):
        return pltpu.make_async_remote_copy(
            src_ref=best.at[column, half, line], dst_ref=taken.at[x, z], send_sem=out_send, recv_sem=out_recv,
            device_id=device(column, y, line + NX * half, c), device_id_type=MESH)

    def back_copy(column, half):
        return pltpu.make_async_remote_copy(
            src_ref=means.at[column, half], dst_ref=back.at[z], send_sem=back_send, recv_sem=back_recv,
            device_id=device(y, column, x + NX * c, half), device_id_type=MESH)

    def finish_step(core, oy):
        column, half = group_place(core, oy)
        mean = jnp.zeros((2 * NZ, SLOTS), jnp.float32)
        number = count[...]
        for line in range(NX):
            for b in range(2):
                top = jnp.where(lane < KEEP, best[column, half, line, b], 0.0)
                value = jnp.sum(top, axis=1, keepdims=True) / number
                best[column, half, line, b] = jnp.where(lane == SLOTS - 1, value, top)
                mean = jnp.where(lane == 2 * line + b, value, mean)
        means[column, half] = mean

    def ship_step(core, oy):
        column, half = group_place(core, oy)
        for line in range(NX):
            here = jnp.logical_and(column == x, line + NX * half == z)

            @pl.when(jnp.logical_not(here))
            def _():
                out_copy(column, line, half).start()

            @pl.when(here)
            def _():
                pltpu.make_async_copy(best.at[column, half, line], taken.at[x, z], out_recv).start()

        here = jnp.logical_and(special, jnp.logical_and(column == y, half == c))

        @pl.when(jnp.logical_not(here))
        def _():
            back_copy(column, half).start()

        @pl.when(here)
        def _():
            pltpu.make_async_copy(means.at[column, half], back.at[z], back_recv).start()

    handlers = {"send": send_event, "arrive": arrive_event, "to_twin": to_twin_event, "twin": twin_event,
                "block": lambda shard, tiles: block_step(*shard, tiles), "finish": lambda group: finish_step(*group), "ship": lambda group: ship_step(*group)}
    for entry in plan()[0]:
        handlers[entry[0]](*entry[1:])

    arrived(back, back_recv)
    arrived(taken, out_recv)
    for link, keys in LINKS.items():
        for i in range(max(len(keys) - WINDOW, 0), len(keys)):
            link_copy(link, i).wait_send()
    arrived(cols.at[0:NY // 2], twin_send)
    arrived(taken.at[0:NX - 1], out_send)
    arrived(taken.at[NX - 1, 0:NZ - 1], out_send)
    arrived(back.at[0:NZ - 1], back_send)

    @pl.when(jnp.logical_not(special))
    def _():
        arrived(back.at[0], back_send)


def place_kernel(taken, back, out, chamfer, turned, mean):
    lane = lax.broadcasted_iota(jnp.int32, (1, SLOTS), 1)
    for k in range(NZ):
        turned[...] = back[k].T
        for i in range(NX):
            mean[pl.ds(16 * i + 2 * k, 2), 0:16] = turned[pl.ds(2 * i, 2), :]
    for i in range(NX):
        line = jnp.zeros((16, SLOTS), jnp.float32)
        for k in range(NZ):
            for b in range(2):
                value = taken[i, k, b]
                line = jnp.where(lane == 2 * k + b, value[:, SLOTS - 1:SLOTS], line)
                out[pl.ds(16 * i, 16), 2 * k + b, :] = jnp.where(lane < KEEP, value, 0.0)
        part = pl.ds(16 * i, 16)
        mean[part, 0:16] = 0.5 * (mean[part, 0:16] + line[:, 0:16])
    chamfer[...] = mean[:, 0:16].T


def on_device(features, tile_counts, projection):
    dma = pltpu.SemaphoreType.DMA
    width = projection.shape[1]
    vmem = pl.BlockSpec(memory_space=pltpu.VMEM)
    anywhere = pl.BlockSpec(memory_space=pl.ANY)
    sends = sum(len(keys) for keys in LINKS.values())
    f32 = jnp.float32
    taken, back = pl.pallas_call(
        kernel,
        name="compare",
        out_shape=(jax.ShapeDtypeStruct((NX, NZ, 2, 16, SLOTS), f32), jax.ShapeDtypeStruct((NZ, 16, SLOTS), f32)),
        in_specs=[anywhere, pl.BlockSpec(memory_space=pltpu.SMEM), anywhere],
        out_specs=(vmem, vmem),
        scratch_shapes=[
            pltpu.VMEM(features.shape, jnp.bfloat16),
            pltpu.VMEM(projection.shape, jnp.bfloat16),
            pltpu.VMEM((SHARD, width), f32),
            pltpu.VMEM((NZ, 2, SLOTS, width), jnp.bfloat16),
            pltpu.VMEM((NY, NX, 2, SHARD, width), jnp.bfloat16),
            pltpu.VMEM((NY, 2, NX, 2, 16, SLOTS), f32),
            pltpu.VMEM((16, SLOTS), f32),
            pltpu.VMEM((NY, 2, 16, SLOTS), f32),
            dma((2,)), dma((sends,)), dma((sends,)), dma, dma((32,)), dma, dma, dma, dma,
        ],
        compiler_params=pltpu.CompilerParams(collective_id=0, has_side_effects=True, vmem_limit_bytes=56 * 2**20),
    )(features, tile_counts, projection)
    out, chamfer = pl.pallas_call(
        place_kernel,
        name="place",
        out_shape=(jax.ShapeDtypeStruct((64, 16, SLOTS), f32), jax.ShapeDtypeStruct((16, 64), f32)),
        in_specs=[vmem, vmem],
        out_specs=(vmem, vmem),
        scratch_shapes=[pltpu.VMEM((SLOTS, 16), f32), pltpu.VMEM((64, SLOTS), f32)],
    )(taken, back)
    return out, chamfer.T


def solution(mesh):
    return jax.shard_map(
        on_device,
        mesh=mesh,
        in_specs=(P(("grp", "dev"), None, None), P(("grp", "dev")), P()),
        out_specs=(P("grp", "dev", None), P("grp", "dev")),
        check_vma=False,
    )
```

```python
import jax
import jax.numpy as jnp
from jax import lax
from jax.experimental import pallas as pl
from jax.experimental.pallas import tpu as pltpu
from jax.sharding import PartitionSpec as P

MESH = pl.DeviceIdType.MESH

NX, NY, NZ = 4, 4, 8
SLOTS = 128
KEEP = 120
SHARD = 2 * KEEP
PIECES = ((0, 0, 64), (0, 64, 128), (1, 128, 192), (1, 192, 240))
WAYS = ((0, 128), (128, 240))
QUARTER = 128
WINDOW = 2

T_ROW = 0.019
T_HOP = 2.2
T_TWIN = 2.0
T_TILE, T_BLOCK, T_EVENT = 0.07, 0.1, 0.02
MOST = 4


def per_piece(entries):
    return tuple((p, ox, oy) for way, ox, oy in entries for p, piece in enumerate(PIECES) if piece[0] == way)


PLUS = ((0, 3, 0), (1, 3, 0), (0, 2, 0), (1, 3, 3), (1, 3, 1), (1, 2, 0), (1, 3, 2), (1, 2, 1))
MINUS = ((0, 1, 0), (1, 1, 0), (1, 1, 1), (1, 1, 3), (1, 1, 2), (1, 2, 3), (1, 2, 2))


def swapped(entries):
    return tuple((1 - way, oy, ox) for way, ox, oy in entries)


def ring_order(way):
    quarters = 2 * SLOTS // QUARTER
    whole = [(-way * o, q) for o in (1, 2, 3) for q in range(quarters)]
    return tuple(whole + [(4, q) for q in range(quarters) if (q < quarters // 2) == (way == 1)])


LINKS = {
    (1, 0, 0): tuple(("col", *k) for k in per_piece(PLUS)),
    (-1, 0, 0): tuple(("col", *k) for k in per_piece(MINUS)),
    (0, 1, 0): tuple(("col", *k) for k in per_piece(swapped(PLUS))),
    (0, -1, 0): tuple(("col", *k) for k in per_piece(swapped(MINUS))),
    (0, 0, 1): tuple(("row", *k) for k in ring_order(1)),
    (0, 0, -1): tuple(("row", *k) for k in ring_order(-1)),
}


def at_sender(link, key):
    dx, dy, dz = link
    if key[0] == "row":
        offset = key[1] + dz
        return ("row", offset - NZ if offset > 4 else offset, key[2])
    return ("col", key[1], (key[2] + dx) % NX, (key[3] + dy) % NY)


def length(key):
    return QUARTER if key[0] == "row" else PIECES[key[1]][2] - PIECES[key[1]][1]


def transfers():
    time = {("row", 0, q): 0.0 for q in range(2 * SLOTS // QUARTER)}
    time.update({("col", p, 0, 0): 0.0 for p in range(len(PIECES))})
    sent = {link: [] for link in LINKS}
    actions = []
    while True:
        nearest = None
        for link, keys in LINKS.items():
            i = len(sent[link])
            if i == len(keys) or at_sender(link, keys[i]) not in time:
                continue
            start = max(time[at_sender(link, keys[i])], sent[link][i - WINDOW] if i >= WINDOW else 0.0)
            if nearest is None or start < nearest[0]:
                nearest = (start, link, i)
        if nearest is None:
            return actions, time
        start, link, i = nearest
        key = LINKS[link][i]
        end = max(start, sent[link][-1] if sent[link] else 0.0) + length(key) * T_ROW
        sent[link].append(end)
        time[key] = end + T_HOP
        actions.append((start, 1, "send", (link, i)))
        actions.append((time[key], 0, "arrive", (link, i)))


def plan():
    events, time = transfers()
    ready = {}
    for ox in range(NX):
        for oy in range(NY):
            for way in range(2):
                t = max(time[("col", p, ox, oy)] for p, piece in enumerate(PIECES) if piece[0] == way)
                twin = (-ox % NX, -oy % NY)
                events.append((t, 2, "to_twin", (way, ox, oy)))
                events.append((t + T_TWIN, 0, "twin", (way, *twin)))
                ready[(0, ox, oy)] = max(ready.get((0, ox, oy), 0.0), t)
                ready[(1, *twin)] = max(ready.get((1, *twin), 0.0), t + T_TWIN)
    tile_ready = {tile: max(time[("row", tile, q)] for q in range(2 * SLOTS // QUARTER)) for tile in range(-3, 5)}
    events.sort(key=lambda e: e[:2])
    todo = {shard: set(tile_ready) for shard in ready}
    order = [(core, oy) for oy in (0, 3, 1, 2) for core in (0, 1)]
    program, now, late = [], 0.0, []
    while events or todo:
        while events and events[0][0] <= now:
            program.append((events[0][2], *events.pop(0)[3]))
            now += T_EVENT
        best = None
        for shard, tiles in todo.items():
            if ready[shard] > now:
                continue
            usable = sorted(t for t in tiles if tile_ready[t] <= now)
            if not usable or (len(usable) < 2 and len(usable) < len(tiles)):
                continue
            if events:
                usable = usable[:MOST]
            rank = (len(usable) == len(tiles), -order.index((shard[0], shard[2])), len(usable))
            if best is None or rank > best[0]:
                best = (rank, shard, usable)
        if best is None:
            now = max(now, events[0][0])
            continue
        _, shard, usable = best
        program.append(("block", shard, tuple(usable)))
        now += T_BLOCK + T_TILE * len(usable)
        todo[shard] -= set(usable)
        if not todo[shard]:
            del todo[shard]
        if late:
            program.append(("ship", late.pop()))
        group = shard[0], shard[2]
        if not any((core, oy) == group for core, _, oy in todo):
            program.append(("finish", group))
            late.append(group)
            now += 0.3
    program.append(("ship", late.pop()))
    return program, now


def kernel(features_hbm, counts, projection_hbm, taken, back, features, projection, emb, rows, cols, best, count, means, *sems):
    load, link_send, link_recv, twin_send, twin_recv, out_send, out_recv, back_send, back_recv = sems
    grp, dev = lax.axis_index("grp"), lax.axis_index("dev")
    y, c = grp // 2, grp % 2
    x, z = dev // NZ, dev % NZ
    sign = 1 - 2 * c

    def device(x, y, z, c):
        return (y * 2 + c, x * NZ + z)

    def near(dx=0, dy=0, dz=0):
        return device((x + sign * dx + NX) % NX, (y + sign * dy + NY) % NY, (z + sign * dz + NZ) % NZ, c)

    twin = device(x, y, z, 1 - c)
    special = jnp.logical_and(z == x + NX * c, x == y)

    barrier = pltpu.get_barrier_semaphore()

    def greet(target):
        pl.semaphore_signal(barrier, inc=1, device_id=target, device_id_type=MESH)

    def back_source(k):
        return jnp.logical_and(special, z == k)

    load_features = pltpu.make_async_copy(features_hbm, features, load.at[0])
    load_projection = pltpu.make_async_copy(projection_hbm, projection, load.at[1])
    load_features.start()
    load_projection.start()
    for k in range(NZ):
        @pl.when(jnp.logical_not(back_source(k)))
        def _():
            greet(device(z % NX, x, k, z // NX))

    for dx in range(NX):
        for dz in range(NZ):
            if (dx, dz) != (0, 0):
                greet(device((x + dx) % NX, y, (z + dz) % NZ, c))
    greet(near(0, 1, 0))
    greet(near(0, -1, 0))
    greet(twin)

    load_features.wait()
    load_projection.wait()

    raw = jnp.dot(features[...].reshape(2 * SLOTS, -1), projection[...], preferred_element_type=jnp.float32)
    scale = lax.rsqrt(jnp.sum(raw * raw, axis=1, keepdims=True) + 1e-06)
    embed = (raw * scale).astype(jnp.bfloat16).astype(jnp.float32)
    slot = lax.broadcasted_iota(jnp.int32, (SLOTS, 1), 0)
    for s in range(2):
        block = embed[s * SLOTS:(s + 1) * SLOTS]
        valid = slot < counts[s]
        number = jnp.where(slot == SLOTS - 1, counts[s].astype(jnp.float32), 0.0)
        rows[z, s] = jnp.where(valid, block, number).astype(jnp.bfloat16)
        emb[pl.ds(s * KEEP, KEEP), :] = jnp.where(valid, block, block[0:1])[:KEEP]
    cols[y, x, c] = emb[...].astype(jnp.bfloat16)

    pl.semaphore_wait(barrier, (NX * NZ - 1) + 3 + NZ - special.astype(jnp.int32))

    def arrived(ref, sem):
        pltpu.make_async_copy(ref, ref, sem).wait()

    def place(core, ox, oy):
        return (y + sign * oy + NY) % NY, (x + sign * ox + NX) % NX, (c if core == 0 else 1 - c)

    def piece_ref(key):
        if key[0] == "row":
            return rows.at[(z + sign * key[1] + NZ) % NZ, key[2] * QUARTER // SLOTS, pl.ds(key[2] * QUARTER % SLOTS, QUARTER)]
        _, p, ox, oy = key
        return cols.at[(*place(0, ox, oy), pl.ds(PIECES[p][1], PIECES[p][2] - PIECES[p][1]))]

    number_of = {}
    for link, keys in LINKS.items():
        for i in range(len(keys)):
            number_of[(link, i)] = len(number_of)

    def link_copy(link, i):
        ref = piece_ref(at_sender(link, LINKS[link][i]))
        index = number_of[(link, i)]
        return pltpu.make_async_remote_copy(
            src_ref=ref, dst_ref=ref, send_sem=link_send.at[index], recv_sem=link_recv.at[index], device_id=near(*link), device_id_type=MESH)

    def send_event(link, i):
        if i >= WINDOW:
            link_copy(link, i - WINDOW).wait_send()
        link_copy(link, i).start()

    def arrive_event(link, i):
        arrived(piece_ref(LINKS[link][i]), link_recv.at[number_of[(link, i)]])

    def way_ref(way, core, ox, oy):
        return cols.at[(*place(core, ox, oy), pl.ds(WAYS[way][0], WAYS[way][1] - WAYS[way][0]))]

    def to_twin_event(way, ox, oy):
        index = (way * NX + ox) * NY + oy
        ref = way_ref(way, 0, ox, oy)
        pltpu.make_async_remote_copy(
            src_ref=ref, dst_ref=ref, send_sem=twin_send, recv_sem=twin_recv.at[index], device_id=twin, device_id_type=MESH).start()

    def twin_event(way, ox, oy):
        arrived(way_ref(way, 1, ox, oy), twin_recv.at[(way * NX + -ox % NX) * NY + -oy % NY])

    counted = set()

    def count_rows(tile):
        counted.add(tile)
        ring = (z + sign * tile + NZ) % NZ
        for s in range(2):
            count[pl.ds(2 * ring + s, 1)] = rows[ring, s, pl.ds(SLOTS - 16, 16), 0:SLOTS].astype(jnp.float32)[15:16]

    def block_step(core, ox, oy, tiles):
        column, line, half = place(core, ox, oy)
        block = cols[column, line, half]
        for tile in tiles:
            if tile not in counted:
                count_rows(tile)
            ring = (z + sign * tile + NZ) % NZ
            score = lax.dot_general(block, rows[ring].reshape(2 * SLOTS, -1), (((1,), (1,)), ((), ())), preferred_element_type=jnp.float32)
            for b in range(2):
                top = jnp.max(score[b * KEEP:(b + 1) * KEEP], axis=0, keepdims=True)
                for s in range(2):
                    best[column, half, line, b, pl.ds(2 * ring + s, 1)] = top[:, s * SLOTS:(s + 1) * SLOTS]

    lane = lax.broadcasted_iota(jnp.int32, (1, SLOTS), 1)

    def group_place(core, oy):
        column, _, half = place(core, 0, oy)
        return column, half

    def out_copy(column, line, half):
        return pltpu.make_async_remote_copy(
            src_ref=best.at[column, half, line], dst_ref=taken.at[x, z], send_sem=out_send, recv_sem=out_recv,
            device_id=device(column, y, line + NX * half, c), device_id_type=MESH)

    def back_copy(column, half):
        return pltpu.make_async_remote_copy(
            src_ref=means.at[column, half], dst_ref=back.at[z], send_sem=back_send, recv_sem=back_recv,
            device_id=device(y, column, x + NX * c, half), device_id_type=MESH)

    def finish_step(core, oy):
        column, half = group_place(core, oy)
        mean = jnp.zeros((2 * NZ, SLOTS), jnp.float32)
        number = count[...]
        for line in range(NX):
            for b in range(2):
                top = jnp.where(lane < KEEP, best[column, half, line, b], 0.0)
                value = jnp.sum(top, axis=1, keepdims=True) / number
                best[column, half, line, b] = jnp.where(lane == SLOTS - 1, value, top)
                mean = jnp.where(lane == 2 * line + b, value, mean)
        means[column, half] = mean

    def ship_step(core, oy):
        column, half = group_place(core, oy)
        for line in range(NX):
            here = jnp.logical_and(column == x, line + NX * half == z)

            @pl.when(jnp.logical_not(here))
            def _():
                out_copy(column, line, half).start()

            @pl.when(here)
            def _():
                pltpu.make_async_copy(best.at[column, half, line], taken.at[x, z], out_recv).start()

        here = jnp.logical_and(special, jnp.logical_and(column == y, half == c))

        @pl.when(jnp.logical_not(here))
        def _():
            back_copy(column, half).start()

        @pl.when(here)
        def _():
            pltpu.make_async_copy(means.at[column, half], back.at[z], back_recv).start()

    handlers = {"send": send_event, "arrive": arrive_event, "to_twin": to_twin_event, "twin": twin_event,
                "block": lambda shard, tiles: block_step(*shard, tiles), "finish": lambda group: finish_step(*group), "ship": lambda group: ship_step(*group)}
    for entry in plan()[0]:
        handlers[entry[0]](*entry[1:])

    arrived(back, back_recv)
    arrived(taken, out_recv)
    for link, keys in LINKS.items():
        for i in range(max(len(keys) - WINDOW, 0), len(keys)):
            link_copy(link, i).wait_send()
    arrived(cols.at[0:NY // 2], twin_send)
    arrived(taken.at[0:NX - 1], out_send)
    arrived(taken.at[NX - 1, 0:NZ - 1], out_send)
    arrived(back.at[0:NZ - 1], back_send)

    @pl.when(jnp.logical_not(special))
    def _():
        arrived(back.at[0], back_send)


def place_kernel(taken, back, out, chamfer, turned, mean):
    lane = lax.broadcasted_iota(jnp.int32, (1, SLOTS), 1)
    for k in range(NZ):
        turned[...] = back[k].T
        for i in range(NX):
            mean[pl.ds(16 * i + 2 * k, 2), 0:16] = turned[pl.ds(2 * i, 2), :]
    for i in range(NX):
        line = jnp.zeros((16, SLOTS), jnp.float32)
        for k in range(NZ):
            for b in range(2):
                value = taken[i, k, b]
                line = jnp.where(lane == 2 * k + b, value[:, SLOTS - 1:SLOTS], line)
                out[pl.ds(16 * i, 16), 2 * k + b, :] = jnp.where(lane < KEEP, value, 0.0)
        part = pl.ds(16 * i, 16)
        mean[part, 0:16] = 0.5 * (mean[part, 0:16] + line[:, 0:16])
    chamfer[...] = mean[:, 0:16].T


def on_device(features, tile_counts, projection):
    dma = pltpu.SemaphoreType.DMA
    width = projection.shape[1]
    vmem = pl.BlockSpec(memory_space=pltpu.VMEM)
    anywhere = pl.BlockSpec(memory_space=pl.ANY)
    sends = sum(len(keys) for keys in LINKS.values())
    f32 = jnp.float32
    taken, back = pl.pallas_call(
        kernel,
        name="compare",
        out_shape=(jax.ShapeDtypeStruct((NX, NZ, 2, 16, SLOTS), f32), jax.ShapeDtypeStruct((NZ, 16, SLOTS), f32)),
        in_specs=[anywhere, pl.BlockSpec(memory_space=pltpu.SMEM), anywhere],
        out_specs=(vmem, vmem),
        scratch_shapes=[
            pltpu.VMEM(features.shape, jnp.bfloat16),
            pltpu.VMEM(projection.shape, jnp.bfloat16),
            pltpu.VMEM((SHARD, width), f32),
            pltpu.VMEM((NZ, 2, SLOTS, width), jnp.bfloat16),
            pltpu.VMEM((NY, NX, 2, SHARD, width), jnp.bfloat16),
            pltpu.VMEM((NY, 2, NX, 2, 16, SLOTS), f32),
            pltpu.VMEM((16, SLOTS), f32),
            pltpu.VMEM((NY, 2, 16, SLOTS), f32),
            dma((2,)), dma((sends,)), dma((sends,)), dma, dma((32,)), dma, dma, dma, dma,
        ],
        compiler_params=pltpu.CompilerParams(collective_id=0, has_side_effects=True, vmem_limit_bytes=56 * 2**20),
    )(features, tile_counts, projection)
    out, chamfer = pl.pallas_call(
        place_kernel,
        name="place",
        out_shape=(jax.ShapeDtypeStruct((64, 16, SLOTS), f32), jax.ShapeDtypeStruct((16, 64), f32)),
        in_specs=[vmem, vmem],
        out_specs=(vmem, vmem),
        scratch_shapes=[pltpu.VMEM((SLOTS, 16), f32), pltpu.VMEM((64, SLOTS), f32)],
    )(taken, back)
    return out, chamfer.T


def solution(mesh):
    return jax.shard_map(
        on_device,
        mesh=mesh,
        in_specs=(P(("grp", "dev"), None, None), P(("grp", "dev")), P()),
        out_specs=(P("grp", "dev", None), P("grp", "dev")),
        check_vma=False,
    )
```
